512 devices in a mesh: blk: 256 (over z, y_lo, x, core), rep: 2 (over y_hi).
Axes of the slice: x: 4, y: 4 (y_hi: 2, y_lo: 2; y = y_hi * 2 + y_lo), z: 16, core: 2. Of those that a mesh axis runs over, the one named last changes fastest.
Arguments:
- residue_string_vectors: float32 [65536, 1024], P(('blk', 'rep')), may hold values from -0.1875 to 0.1875
- fold_shape_vectors: float32 [65536, 1024], P('blk'), may hold values from -0.1875 to 0.1875
- family_label: int32 [65536], P('blk'), may hold values from 0 to 2047, as said below
- sharpness_multiplier: float32 [1], replicated, may hold values from 4 to 12
- additive_offset_term: float32 [1], replicated, may hold values from -5 to -2
Outputs:
- loss_rows: float32 [65536], P(('blk', 'rep'))
- sequence_gradient: float32 [65536, 1024], P(('blk', 'rep'))
- structure_gradient: float32 [65536, 1024], P('blk')
The draws below stay inside these ranges and needn't reach their ends.
Inputs may be any that keep to these rules, and one draw needn't show every extreme that they name: `family_label`: members of one cluster lie in blocks at most 8 apart along the loop of 256 blocks.
All inputs are finite; a program needn't handle non-finite values.
Results may differ from the reference program's by a relative error of at most 0.0003.
Values sent between devices are 32-bit elements; how exact they have to be, the bound alone decides.
A program may use at most 64 MiB of HBM per device.

```python
import math
import jax
import jax.numpy as jnp
from jax import lax

FEATURE_SPAN = 1024
B_DEV = 256
HOPS = 4
GROUPS = 8
BLOCKS = 256
MOLECULE_TALLY = 65536


def draw_family_label(key, part):
    key = jax.random.fold_in(key, 7)
    first_key, second_key = jax.random.split(key)
    positions = jnp.arange(MOLECULE_TALLY, dtype=jnp.int32)
    home_block = positions // B_DEV
    reach = jax.random.randint(first_key, (MOLECULE_TALLY,), 0, HOPS + 1).astype(jnp.int32)
    member = jax.random.randint(second_key, (MOLECULE_TALLY,), 0, GROUPS).astype(jnp.int32)
    anchor = (home_block + 2 * reach) % BLOCKS
    return (anchor * GROUPS + member).astype(jnp.int32)


def block_levels(key, dims, cuts, smallest, top_value):
    gain, own = 1.0, jax.random.fold_in(key, 6)
    for position, parts in cuts:
        heights = jnp.exp(jax.random.uniform(jax.random.fold_in(own, position), (parts,), jnp.float32, smallest / len(cuts), top_value / len(cuts)))
        gain = gain * jnp.repeat(heights, dims[position] // parts).reshape([-1 if axis == position else 1 for axis in range(len(dims))])
    return gain


def centred(stream_key, shape, width, most, pieces=(), kind=jnp.bfloat16):
    drawn = jax.random.normal(stream_key, shape, jnp.float32) * width
    if len(pieces) > 0:
        drawn = block_levels(stream_key, shape, pieces, -0.22, 0.18) * drawn
    return jnp.clip(drawn, min=-most, max=most).astype(kind)


def setup_inputs(seed: int = 0) -> dict:
    key_list = jax.random.split(jax.random.key(seed), 6)
    return {
        "residue_string_vectors": centred(key_list[0], (MOLECULE_TALLY, FEATURE_SPAN), 0.03125, 0.1875, ((0, 512),), jnp.float32),
        "fold_shape_vectors": centred(key_list[1], (MOLECULE_TALLY, FEATURE_SPAN), 0.03125, 0.1875, ((0, 256),), jnp.float32),
        "family_label": draw_family_label(jax.random.fold_in(key_list[5], 71), 0),
        "sharpness_multiplier": jnp.clip(jnp.exp(jax.random.uniform(key_list[3], (1,), jnp.float32, math.log(4.0), math.log(12.0))), 4.0, 12.0),
        "additive_offset_term": jnp.clip(jax.random.uniform(key_list[4], (1,), jnp.float32, -5.0, -2.0), -5.0, -2.0),
    }


EPSILON = 1e-06

def unit_rows(embedding):
    length = jnp.sqrt(lax.optimization_barrier(jnp.sum(embedding * embedding, axis=-1, keepdims=True)) + EPSILON)
    return (embedding / length, length)

def project_tangent(direction, unit, length):
    along = lax.optimization_barrier(jnp.sum(unit * direction, axis=-1, keepdims=True))
    return (direction - unit * along) / length

def reference(residue_string_vectors, fold_shape_vectors, family_label, sharpness_multiplier, additive_offset_term):
    residue_string_unitized, residue_string_length = unit_rows(residue_string_vectors)
    fold_shape_unitized, fold_shape_length = unit_rows(fold_shape_vectors)
    seq_blocks = residue_string_unitized.reshape(BLOCKS, B_DEV, FEATURE_SPAN)
    struct_blocks = fold_shape_unitized.reshape(BLOCKS, B_DEV, FEATURE_SPAN)
    cluster_blocks = family_label.reshape(BLOCKS, B_DEV)
    loss_sum = jnp.zeros((BLOCKS, B_DEV), jnp.float32)
    residue_string_accumulated = jnp.zeros((BLOCKS, B_DEV, FEATURE_SPAN), jnp.float32)
    fold_shape_accumulated = jnp.zeros((BLOCKS, B_DEV, FEATURE_SPAN), jnp.float32)
    for stride in range(HOPS + 1):
        partner = jnp.roll(struct_blocks, -2 * stride, axis=0)
        partner_ids = jnp.roll(cluster_blocks, -2 * stride, axis=0)
        angular_similarity_grid = jnp.einsum('bid,bjd->bij', seq_blocks, partner, precision=lax.Precision.HIGHEST)
        score_grid = sharpness_multiplier[0] * angular_similarity_grid + additive_offset_term[0]
        agreement = 2.0 * (cluster_blocks[:, :, None] == partner_ids[:, None, :]).astype(jnp.float32) - 1.0
        margin = -agreement * score_grid
        loss_sum = loss_sum + lax.optimization_barrier(jnp.sum(jax.nn.softplus(margin), axis=2))
        weight = -agreement * jax.nn.sigmoid(margin)
        residue_string_accumulated = residue_string_accumulated + jnp.einsum('bij,bjd->bid', weight, partner, precision=lax.Precision.HIGHEST)
        struct_part = jnp.einsum('bij,bid->bjd', weight, seq_blocks, precision=lax.Precision.HIGHEST)
        fold_shape_accumulated = fold_shape_accumulated + jnp.roll(struct_part, 2 * stride, axis=0)
    residue_string_direction = sharpness_multiplier[0] * residue_string_accumulated.reshape(MOLECULE_TALLY, FEATURE_SPAN)
    fold_shape_direction = sharpness_multiplier[0] * fold_shape_accumulated.reshape(MOLECULE_TALLY, FEATURE_SPAN)
    loss_rows = loss_sum.reshape(MOLECULE_TALLY) / ((HOPS + 1) * B_DEV)
    sequence_gradient = project_tangent(residue_string_direction, residue_string_unitized, residue_string_length)
    structure_gradient = project_tangent(fold_shape_direction, fold_shape_unitized, fold_shape_length)
    return (loss_rows, sequence_gradient, structure_gradient)
```

```python
import functools

import jax
import jax.numpy as jnp
from jax import lax
from jax.experimental import pallas as pl
from jax.experimental.pallas import tpu as pltpu
from jax.sharding import PartitionSpec as P

MESH = pl.DeviceIdType.MESH
HOPS = 4
EPSILON = 1e-06
CHUNKS = 4
RING = 4
TILES = (1, 3, 2)


def split(value):
    high = value.astype(jnp.bfloat16)
    return high, (value - high.astype(jnp.float32)).astype(jnp.bfloat16)


def dot3(a, b, dims):
    def one(p, q):
        return lax.dot_general(p, q, (dims, ((), ())), preferred_element_type=jnp.float32)

    return one(a[0], b[0]) + one(a[0], b[1]) + one(a[1], b[0])


def unit_of(raw):
    length = jnp.sqrt(jnp.sum(raw * raw, axis=1, keepdims=True) + EPSILON)
    return raw / length, length


def project(direction, raw):
    unit, length = unit_of(raw)
    along = jnp.sum(unit * direction, axis=1, keepdims=True)
    return (direction - unit * along) / length


def kernel(
    groups,
    seq_hbm,
    st_hbm,
    lab_ref,
    scale_ref,
    bias_ref,
    loss_out,
    seq_out,
    st_out,
    seqv,
    units,
    labs,
    parts,
    backs,
    cross_back,
    acc,
    seq_part,
    loss_mine,
    loss_part,
    final,
    sq_hi,
    sq_lo,
    load_sem,
    seq_sems,
    loss_sems,
    sp_sems,
    cross_s,
    cross_r,
    ring_s,
    ring_r,
    lab_s,
    lab_r,
    back_s,
    back_r,
    xback_s,
    xback_r,
    final_s,
    final_r,
):
    half = seq_hbm.shape[0]
    rows = half // CHUNKS
    blk, rep = lax.axis_index("blk"), lax.axis_index("rep")
    core, x, group = blk % 2, (blk // 2) % RING, blk // (2 * RING)

    def at(g, column, replica):
        return ((lax.rem(g + groups, groups) * RING + lax.rem(column + RING, RING)) * 2 + core, replica)

    def ring(by):
        return at(group, x + by, rep)

    up = at(group + 1, x, lax.rem(rep + group + core, 2))
    down = at(group - 1, x, lax.rem(rep + group + 1 + core, 2))
    partner = (blk, 1 - rep)

    def send(src, dst, send_sem, recv_sem, device):
        return pltpu.make_async_remote_copy(
            src_ref=src, dst_ref=dst, send_sem=send_sem, recv_sem=recv_sem, device_id=device, device_id_type=MESH
        )

    def part(k):
        return pl.ds(k * rows, rows)

    mine = pl.multiple_of(rep * half, half)

    def source(k):
        return st_hbm.at[pl.ds(mine + k * rows, rows)]

    def cross_copy(k):
        return send(source(k), units.at[HOPS, part(k)], cross_s.at[k], cross_r.at[k], down)

    def ring_copy(h, k, crossed):
        src = units.at[HOPS, part(k)] if crossed else source(k)
        return send(src, units.at[h, part(k)], ring_s.at[h - 1, k], ring_r.at[h - 1, k], ring(-h))

    def label_copy(h, crossed):
        src = labs.at[HOPS if crossed else 0]
        return send(src, labs.at[h], lab_s.at[h - 1], lab_r.at[h - 1], down if h == HOPS else ring(-h))

    def back_copy(h, k):
        return send(parts.at[h, part(k)], backs.at[h - 1, part(k)], back_s.at[h - 1, k], back_r.at[h - 1, k], ring(h))

    def cross_back_copy(k):
        return send(parts.at[HOPS, part(k)], cross_back.at[part(k)], xback_s.at[k], xback_r.at[k], up)

    def final_copy(k):
        return send(parts.at[0, part(k)], final.at[part(k)], final_s.at[k], final_r.at[k], partner)

    seq_copy = send(seq_hbm, seqv.at[pl.ds(half, half)], seq_sems.at[0], seq_sems.at[1], partner)
    seq_part_copy = send(acc.at[pl.ds(half, half)], seq_part, sp_sems.at[0], sp_sems.at[1], partner)
    loss_copy = send(loss_mine, loss_part, loss_sems.at[0], loss_sems.at[1], partner)

    load_seq = pltpu.make_async_copy(seq_hbm, seqv.at[pl.ds(0, half)], load_sem.at[0])
    load_st = pltpu.make_async_copy(st_hbm.at[pl.ds(mine, half)], units.at[0], load_sem.at[1])
    load_seq.start()
    load_st.start()

    barrier = pltpu.get_barrier_semaphore()
    for device in (ring(1), ring(2), ring(3), up, down, partner):
        pl.semaphore_signal(barrier, 1, device_id=device, device_id_type=MESH)
    my_labels = lab_ref[pl.ds(rep, 1), :]
    other_labels = lab_ref[pl.ds(1 - rep, 1), :]
    labs[0] = jnp.broadcast_to(my_labels, (8, half))
    pl.semaphore_wait(barrier, 6)

    for k in range(CHUNKS):
        cross_copy(k).start()
    label_copy(HOPS, False).start()
    for h in TILES:

        @pl.when(x >= h)
        def _():
            for k in range(CHUNKS):
                ring_copy(h, k, False).start()
            label_copy(h, False).start()

    seq_copy.start()

    load_seq.wait()
    unit, _ = unit_of(seqv[pl.ds(0, half)])
    sq_hi[pl.ds(0, half)], sq_lo[pl.ds(0, half)] = split(unit)
    load_st.wait()

    for k in range(CHUNKS):
        cross_copy(k).wait_recv()
        for h in TILES:

            @pl.when(x < h)
            def _():
                ring_copy(h, k, True).start()

    label_copy(HOPS, False).wait_recv()
    for h in TILES:

        @pl.when(x < h)
        def _():
            label_copy(h, True).start()

    seq_copy.wait_recv()
    unit, _ = unit_of(seqv[pl.ds(half, half)])
    sq_hi[pl.ds(half, half)], sq_lo[pl.ds(half, half)] = split(unit)

    scale, bias = scale_ref[0], bias_ref[0]

    def tile(h, first, loss):
        st = split(unit_of(units[h])[0])
        sq = (sq_hi[...], sq_lo[...])
        logit = scale * dot3(st, sq, ((1,), (1,))) + bias
        label = jnp.broadcast_to(labs[h][0:1, :].astype(jnp.float32), (half, half)).T
        match = jnp.concatenate(
            [label == my_labels.astype(jnp.float32), label == other_labels.astype(jnp.float32)], axis=1
        )
        margin = jnp.where(match, -logit, logit)
        small = jnp.exp(-jnp.abs(margin))
        loss = loss + jnp.sum(jnp.maximum(margin, 0.0) + jnp.log1p(small), axis=0, keepdims=True)
        sigmoid = jnp.where(margin >= 0.0, 1.0, small) / (1.0 + small)
        weight = jnp.where(match, -sigmoid, sigmoid)
        parts[h] = dot3(split(weight), sq, ((1,), (0,)))
        towards = dot3(split(weight.T), st, ((1,), (0,)))
        if first:
            acc[...] = towards
        else:
            acc[...] += towards
        return loss

    loss = jnp.zeros((1, 2 * half), jnp.float32)
    loss = tile(0, True, loss)
    loss = tile(HOPS, False, loss)
    for h in TILES:
        for k in range(CHUNKS):
            ring_copy(h, k, False).wait_recv()
        label_copy(h, False).wait_recv()
        loss = tile(h, False, loss)
        for k in range(CHUNKS):
            back_copy(h, k).start()

    seq_part_copy.start()
    loss_mine[...] = jnp.broadcast_to(loss[:, half:], (8, half))
    loss_copy.start()

    def collect(k):
        for h in TILES:

            @pl.when(x < h)
            def _():
                back_copy(h, k).wait_recv()
                parts[HOPS, part(k)] += backs[h - 1, part(k)]

        cross_back_copy(k).start()

    def finish(k):
        for h in TILES:

            @pl.when(x >= h)
            def _():
                back_copy(h, k).wait_recv()
                parts[0, part(k)] += backs[h - 1, part(k)]

        cross_back_copy(k).wait_recv()
        direction = scale * (parts[0, part(k)] + cross_back[part(k)])
        done = project(direction, units[0, part(k)])
        parts[0, part(k)] = done
        final_copy(k).start()
        st_out[pl.ds(mine + k * rows, rows)] = done

    for k in range(CHUNKS + 1):
        if k < CHUNKS:
            collect(k)
        if k > 0:
            finish(k - 1)

    loss_copy.wait_recv()
    loss_out[...] = (loss[:, :half] + loss_part[0:1, :]) / ((HOPS + 1) * 2.0 * half)
    seq_part_copy.wait_recv()
    seq_out[...] = project(scale * (acc[pl.ds(0, half)] + seq_part[...]), seqv[pl.ds(0, half)])

    theirs = pl.multiple_of((1 - rep) * half, half)
    for k in range(CHUNKS):
        final_copy(k).wait_recv()
        st_out[pl.ds(theirs + k * rows, rows)] = final[part(k)]

    for k in range(CHUNKS):
        cross_copy(k).wait_send()
        cross_back_copy(k).wait_send()
        final_copy(k).wait_send()
        for h in TILES:
            ring_copy(h, k, False).wait_send()
            back_copy(h, k).wait_send()
    for h in TILES + (HOPS,):
        label_copy(h, False).wait_send()
    seq_copy.wait_send()
    seq_part_copy.wait_send()
    loss_copy.wait_send()


def body(seq, st, label, scale, bias):
    half, features = seq.shape
    f32, bf16 = jnp.float32, jnp.bfloat16
    vmem, dma = pltpu.VMEM, pltpu.SemaphoreType.DMA
    groups = lax.axis_size("blk") // (2 * RING)
    loss, seq_grad, st_grad = pl.pallas_call(
        functools.partial(kernel, groups),
        out_shape=(
            jax.ShapeDtypeStruct((1, half), f32),
            jax.ShapeDtypeStruct(seq.shape, f32),
            jax.ShapeDtypeStruct(st.shape, f32),
        ),
        in_specs=[
            pl.BlockSpec(memory_space=pl.ANY),
            pl.BlockSpec(memory_space=pl.ANY),
            pl.BlockSpec(memory_space=vmem),
            pl.BlockSpec(memory_space=pltpu.SMEM),
            pl.BlockSpec(memory_space=pltpu.SMEM),
        ],
        out_specs=(pl.BlockSpec(memory_space=vmem),) * 3,
        scratch_shapes=[
            vmem((2 * half, features), f32),
            vmem((HOPS + 1, half, features), f32),
            vmem((HOPS + 1, 8, half), jnp.int32),
            vmem((HOPS + 1, half, features), f32),
            vmem((RING - 1, half, features), f32),
            vmem((half, features), f32),
            vmem((2 * half, features), f32),
            vmem((half, features), f32),
            vmem((8, half), f32),
            vmem((8, half), f32),
            vmem((half, features), f32),
            vmem((2 * half, features), bf16),
            vmem((2 * half, features), bf16),
            dma((2,)),
            dma((2,)),
            dma((2,)),
            dma((2,)),
            dma((CHUNKS,)),
            dma((CHUNKS,)),
            dma((RING - 1, CHUNKS)),
            dma((RING - 1, CHUNKS)),
            dma((HOPS,)),
            dma((HOPS,)),
            dma((RING - 1, CHUNKS)),
            dma((RING - 1, CHUNKS)),
            dma((CHUNKS,)),
            dma((CHUNKS,)),
            dma((CHUNKS,)),
            dma((CHUNKS,)),
        ],
        compiler_params=pltpu.CompilerParams(
            collective_id=1, has_side_effects=True, vmem_limit_bytes=56 * 2**20
        ),
    )(seq, st, label.reshape(2, half), scale, bias)
    return loss.reshape(half), seq_grad, st_grad


def solution(mesh):
    placed = (P(("blk", "rep"), None), P("blk", None), P("blk"), P(), P())
    return jax.shard_map(
        body,
        mesh=mesh,
        in_specs=placed,
        out_specs=(P(("blk", "rep")), P(("blk", "rep"), None), P("blk", None)),
        check_vma=False,
    )
```

```python
import functools

import jax
import jax.numpy as jnp
from jax import lax
from jax.experimental import pallas as pl
from jax.experimental.pallas import tpu as pltpu
from jax.sharding import PartitionSpec as P

MESH = pl.DeviceIdType.MESH
HOPS = 4
EPSILON = 1e-06
CHUNKS = 4
RING = 4
TILES = (3, 2, 1)
PIECES = 4
RELAY = True
READY = 4


def split(value):
    high = value.astype(jnp.bfloat16)
    return high, (value - high.astype(jnp.float32)).astype(jnp.bfloat16)


def dot3(a, b, dims):
    def one(p, q):
        return lax.dot_general(p, q, (dims, ((), ())), preferred_element_type=jnp.float32)

    return one(a[0], b[0]) + one(a[0], b[1]) + one(a[1], b[0])


def unit_of(raw):
    length = jnp.sqrt(jnp.sum(raw * raw, axis=1, keepdims=True) + EPSILON)
    inverse = 1.0 / length
    return raw * inverse, inverse


def project(direction, raw):
    unit, inverse = unit_of(raw)
    along = jnp.sum(unit * direction, axis=1, keepdims=True)
    return (direction - unit * along) * inverse


def kernel(
    groups,
    seq_hbm,
    st_hbm,
    lab_ref,
    scale_ref,
    bias_ref,
    loss_hbm,
    seq_out,
    st_out,
    stv,
    units,
    labs,
    columns,
    parts,
    backs,
    cross_back,
    acc,
    acc_in,
    losses,
    loss_backs,
    loss_cross,
    st_hi,
    st_lo,
    load_sem,
    acc_s,
    acc_r,
    cross_s,
    cross_r,
    ring_s,
    ring_r,
    lab_s,
    lab_r,
    back_s,
    back_r,
    xback_s,
    xback_r,
    loss_s,
    loss_r,
    loss_out,
    put_sem,
):
    half, features = seq_hbm.shape
    rows = half // CHUNKS
    piece = 2 * half // PIECES
    blk, rep = lax.axis_index("blk"), lax.axis_index("rep")
    core, x, group = blk % 2, (blk // 2) % RING, blk // (2 * RING)

    def at(g, column, replica):
        return ((lax.rem(g + groups, groups) * RING + lax.rem(column + RING, RING)) * 2 + core, replica)

    def ring(by):
        return at(group, x + by, rep)

    rep_up = lax.rem(rep + group + core, 2)
    rep_down = lax.rem(rep + group + 1 + core, 2)
    up = at(group + 1, x, rep_up)
    down = at(group - 1, x, rep_down)
    wraps = jnp.where(x == RING - 1, 1, 0)
    later = at(group + wraps, x + 1, jnp.where(x == RING - 1, rep_up, rep))
    wraps = jnp.where(x == 0, 1, 0)
    earlier = at(group - wraps, x - 1, jnp.where(x == 0, rep_down, rep))
    partner = (blk, 1 - rep)

    def send(src, dst, send_sem, recv_sem, device):
        return pltpu.make_async_remote_copy(
            src_ref=src, dst_ref=dst, send_sem=send_sem, recv_sem=recv_sem, device_id=device, device_id_type=MESH
        )

    def stays(h):
        return x < RING - h

    def leaves(h):
        return x >= RING - h

    def source(k):
        return seq_hbm.at[pl.ds(k * rows, rows)]

    def cross_copy(k):
        return send(source(k), units.at[k, HOPS], cross_s.at[k], cross_r.at[k], up)

    def ring_copy(h, k, crossed):
        src = units.at[k, HOPS] if crossed else source(k)
        return send(src, units.at[k, h], ring_s.at[h - 1, k], ring_r.at[h - 1, k], ring(h))

    def second_copy(k):
        over = k % 2 == 0
        return send(
            units.at[k, 1 if over else 3], units.at[k, 2], ring_s.at[1, k], ring_r.at[1, k], later if over else earlier
        )

    def label_copy(h, crossed):
        src = labs.at[HOPS if crossed else 0]
        return send(src, labs.at[h], lab_s.at[h - 1], lab_r.at[h - 1], up if h == HOPS else ring(h))

    def back_copy(h, k):
        return send(parts.at[k, h], backs.at[k, h - 1], back_s.at[h - 1, k], back_r.at[h - 1, k], ring(-h))

    def cross_back_copy(k):
        return send(parts.at[k, HOPS], cross_back.at[k], xback_s.at[k], xback_r.at[k], down)

    def loss_copy(h):
        dst = loss_cross if h == HOPS else loss_backs.at[h - 1]
        return send(losses.at[h], dst, loss_s.at[h - 1], loss_r.at[h - 1], down if h == HOPS else ring(-h))

    def acc_copy(p):
        here = pl.ds(p * piece, piece)
        return send(acc.at[here], acc_in.at[here], acc_s.at[p], acc_r.at[p], partner)

    load_st = pltpu.make_async_copy(st_hbm, stv, load_sem.at[0])
    load_seq = [pltpu.make_async_copy(source(k), units.at[k, 0], load_sem.at[1 + k]) for k in range(CHUNKS)]
    load_st.start()
    for copy in load_seq:
        copy.start()

    barrier = pltpu.get_barrier_semaphore()
    greeted = (ring(1), ring(2), ring(3), up, down, partner, later, earlier)
    for device in greeted:
        pl.semaphore_signal(barrier, 1, device_id=device, device_id_type=MESH)
    labs[0] = jnp.broadcast_to(lab_ref[pl.ds(rep, 1), :], (8, half))
    label_rows = [lab_ref[q : q + 1, :].astype(jnp.float32) for q in range(2)]
    pl.semaphore_wait(barrier, len(greeted))

    direct = (1, 3) if RELAY else (1, 3, 2)

    def forward(k):
        for h in direct:

            @pl.when(stays(h))
            def _():
                ring_copy(h, k, False).start()

    def relay(k):
        cross_copy(k).wait_recv()
        for h in direct:

            @pl.when(leaves(h))
            def _():
                ring_copy(h, k, True).start()

    def second(k):
        ring_copy(1 if k % 2 == 0 else 3, k, False).wait_recv()
        second_copy(k).start()

    def arrived(k):
        for h in TILES:
            if not (RELAY and h == (1 if k % 2 == 0 else 3)):
                ring_copy(h, k, False).wait_recv()

    def column(h):
        tall = jnp.broadcast_to(labs[h][0:1, :].astype(jnp.float32), (half, half)).T
        for k in range(CHUNKS):
            columns[k, h] = tall[k * rows : (k + 1) * rows]

    scale, bias = scale_ref[0], bias_ref[0]

    def back(k):
        for h in TILES:
            back_copy(h, k).start()

    def stage(k):
        arrived(k)
        seq = split(unit_of(units[k].reshape((HOPS + 1) * rows, features))[0])
        st = (st_hi[...], st_lo[...])
        logit = scale * dot3(seq, st, ((1,), (1,))) + bias
        label = columns[k].reshape((HOPS + 1) * rows, half)
        match = jnp.concatenate([label == label_rows[0], label == label_rows[1]], axis=1)
        margin = jnp.where(match, -logit, logit)
        small = jnp.exp(-jnp.abs(margin))
        loss = jnp.sum(jnp.maximum(margin, 0.0) + jnp.log1p(small), axis=1, keepdims=True)
        loss = jnp.broadcast_to(loss, label.shape).reshape(HOPS + 1, rows, half)
        columns[k] = loss
        sigmoid = jnp.where(margin >= 0.0, 1.0, small) / (1.0 + small)
        weight = split(jnp.where(match, -sigmoid, sigmoid))
        parts[k] = dot3(weight, st, ((1,), (0,))).reshape(HOPS + 1, rows, features)
        back(k)
        towards = lax.dot_general(
            jnp.concatenate([weight[0], weight[1], weight[0]], axis=0),
            jnp.concatenate([seq[0], seq[0], seq[1]], axis=0),
            (((0,), (0,)), ((), ())),
            preferred_element_type=jnp.float32,
        )
        if k == 0:
            acc[...] = towards
        else:
            acc[...] += towards

    def collect(k):
        for h in TILES:

            @pl.when(leaves(h))
            def _():
                back_copy(h, k).wait_recv()
                parts[k, HOPS] += backs[k, h - 1]

        cross_back_copy(k).start()

    def finish(k):
        for h in TILES:

            @pl.when(stays(h))
            def _():
                back_copy(h, k).wait_recv()
                parts[k, 0] += backs[k, h - 1]

        cross_back_copy(k).wait_recv()
        parts[k, 0] = project(scale * (parts[k, 0] + cross_back[k]), units[k, 0])
        put_seq(k).start()

    put_loss = pltpu.make_async_copy(loss_out, loss_hbm, put_sem.at[0])

    def put_seq(k):
        return pltpu.make_async_copy(parts.at[k, 0], seq_out.at[pl.ds(k * rows, rows)], put_sem.at[1 + k])

    def put_st(p):
        here = pl.ds(p * piece, piece)
        return pltpu.make_async_copy(acc_in.at[here], st_out.at[here], put_sem.at[1 + CHUNKS + p])

    def settle(p):
        here = pl.ds(p * piece, piece)
        acc_copy(p).wait_recv()
        acc_in[here] = project(scale * (acc[here] + acc_in[here]), stv[here])
        put_st(p).start()

    label_copy(HOPS, False).start()
    for h in TILES:

        @pl.when(stays(h))
        def _():
            label_copy(h, False).start()

    for k in range(CHUNKS):
        cross_copy(k).start()
        forward(k)

    column(0)
    load_st.wait()
    unit, _ = unit_of(stv[...])
    st_hi[...], st_lo[...] = split(unit)
    for copy in load_seq:
        copy.wait()
    label_copy(HOPS, False).wait_recv()
    for h in TILES:

        @pl.when(leaves(h))
        def _():
            label_copy(h, True).start()

    column(HOPS)
    for k in range(CHUNKS):
        relay(k)
    for h in TILES:
        label_copy(h, False).wait_recv()
        column(h)
    for k in range(READY if RELAY else 0):
        second(k)
    for k in range(CHUNKS):
        stage(k)
        if RELAY and k + READY < CHUNKS:
            second(k + READY)
    for p in range(PIECES):
        acc_copy(p).start()

    for h in range(HOPS + 1):
        tall = jnp.concatenate([columns[k, h] for k in range(CHUNKS)], axis=0)
        losses[h] = tall.T[0:8, :]
    for h in TILES:
        loss_copy(h).start()
    for k in range(CHUNKS):
        collect(k)
        if k == 1:
            for h in TILES:
                loss_copy(h).wait_recv()
            gone = losses[HOPS]
            kept = losses[0]
            for h in TILES:
                gone += jnp.where(leaves(h), loss_backs[h - 1], 0.0)
                kept += jnp.where(stays(h), loss_backs[h - 1], 0.0)
            losses[HOPS] = gone
            loss_copy(HOPS).start()
    for p in range(PIECES):
        settle(p)
    for k in range(CHUNKS):
        finish(k)
    loss_copy(HOPS).wait_recv()
    loss_out[...] = (kept[0:1, :] + loss_cross[0:1, :]) / ((HOPS + 1) * 2.0 * half)
    put_loss.start()

    for k in range(CHUNKS):
        cross_copy(k).wait_send()
        cross_back_copy(k).wait_send()
        for h in TILES:
            ring_copy(h, k, False).wait_send()
            back_copy(h, k).wait_send()
    for h in TILES + (HOPS,):
        label_copy(h, False).wait_send()
        loss_copy(h).wait_send()
    for p in range(PIECES):
        acc_copy(p).wait_send()
        put_st(p).wait()
    for k in range(CHUNKS):
        put_seq(k).wait()
    put_loss.wait()


def hand_over(a, b, c, p, q, r, sa, sb, sc, sem):
    moves = [(a, sa, p, slice(None)), (b, sb, q, slice(None))]
    half = b.shape[0]
    moves += [(c, sc, r, pl.ds(i * half, half)) for i in range(2)]
    ins = [pltpu.make_async_copy(s.at[w], v.at[w], sem.at[0, i]) for i, (s, v, _, w) in enumerate(moves)]
    outs = [pltpu.make_async_copy(v.at[w], d.at[w], sem.at[1, i]) for i, (_, v, d, w) in enumerate(moves)]
    for copy in ins:
        copy.start()
    for into, out in zip(ins, outs):
        into.wait()
        out.start()
    for copy in outs:
        copy.wait()


def body(seq, st, label, scale, bias):
    half, features = seq.shape
    rows = half // CHUNKS
    f32, bf16 = jnp.float32, jnp.bfloat16
    vmem, dma = pltpu.VMEM, pltpu.SemaphoreType.DMA
    groups = lax.axis_size("blk") // (2 * RING)
    loss, seq_grad, st_grad = pl.pallas_call(
        functools.partial(kernel, groups),
        out_shape=(
            jax.ShapeDtypeStruct((1, half), f32),
            jax.ShapeDtypeStruct(seq.shape, f32),
            jax.ShapeDtypeStruct(st.shape, f32),
        ),
        in_specs=[
            pl.BlockSpec(memory_space=pl.ANY),
            pl.BlockSpec(memory_space=pl.ANY),
            pl.BlockSpec(memory_space=vmem),
            pl.BlockSpec(memory_space=pltpu.SMEM),
            pl.BlockSpec(memory_space=pltpu.SMEM),
        ],
        out_specs=(pl.BlockSpec(memory_space=pl.ANY),) * 3,
        scratch_shapes=[
            vmem((2 * half, features), f32),
            vmem((CHUNKS, HOPS + 1, rows, features), f32),
            vmem((HOPS + 1, 8, half), jnp.int32),
            vmem((CHUNKS, HOPS + 1, rows, half), f32),
            vmem((CHUNKS, HOPS + 1, rows, features), f32),
            vmem((CHUNKS, RING - 1, rows, features), f32),
            vmem((CHUNKS, rows, features), f32),
            vmem((2 * half, features), f32),
            vmem((2 * half, features), f32),
            vmem((HOPS + 1, 8, half), f32),
            vmem((RING - 1, 8, half), f32),
            vmem((8, half), f32),
            vmem((2 * half, features), bf16),
            vmem((2 * half, features), bf16),
            dma((1 + CHUNKS,)),
            dma((PIECES,)),
            dma((PIECES,)),
            dma((CHUNKS,)),
            dma((CHUNKS,)),
            dma((RING - 1, CHUNKS)),
            dma((RING - 1, CHUNKS)),
            dma((HOPS,)),
            dma((HOPS,)),
            dma((RING - 1, CHUNKS)),
            dma((RING - 1, CHUNKS)),
            dma((CHUNKS,)),
            dma((CHUNKS,)),
            dma((HOPS,)),
            dma((HOPS,)),
            vmem((1, half), f32),
            dma((1 + CHUNKS + PIECES,)),
        ],
        compiler_params=pltpu.CompilerParams(
            collective_id=1, has_side_effects=True, vmem_limit_bytes=56 * 2**20
        ),
    )(seq, st, label.reshape(2, half), scale, bias)
    loss, seq_grad, st_grad = pl.pallas_call(
        hand_over,
        out_shape=(
            jax.ShapeDtypeStruct((1, half), f32),
            jax.ShapeDtypeStruct(seq.shape, f32),
            jax.ShapeDtypeStruct(st.shape, f32),
        ),
        in_specs=[pl.BlockSpec(memory_space=pl.ANY)] * 3,
        out_specs=(pl.BlockSpec(memory_space=pl.ANY),) * 3,
        scratch_shapes=[vmem((1, half), f32), vmem(seq.shape, f32), vmem(st.shape, f32), dma((2, 4))],
        name="hand_over",
    )(loss, seq_grad, st_grad)
    return loss.reshape(half), seq_grad, st_grad


def solution(mesh):
    placed = (P(("blk", "rep"), None), P("blk", None), P("blk"), P(), P())
    return jax.shard_map(
        body,
        mesh=mesh,
        in_specs=placed,
        out_specs=(P(("blk", "rep")), P(("blk", "rep"), None), P("blk", None)),
        check_vma=False,
    )
```

```python
import functools

import jax
import jax.numpy as jnp
from jax import lax
from jax.experimental import pallas as pl
from jax.experimental.pallas import tpu as pltpu
from jax.sharding import PartitionSpec as P

MESH = pl.DeviceIdType.MESH
HOPS = 4
EPSILON = 1e-06
CHUNKS = 4
RING = 4
TILES = (3, 2, 1)
PIECES = 4
FINE = 8
FOURTH = 4


def split(value):
    high = value.astype(jnp.bfloat16)
    return high, (value - high.astype(jnp.float32)).astype(jnp.bfloat16)


def dot3(a, b, dims):
    def one(p, q):
        return lax.dot_general(p, q, (dims, ((), ())), preferred_element_type=jnp.float32)

    return one(a[0], b[0]) + one(a[0], b[1]) + one(a[1], b[0])


def unit_of(raw):
    length = jnp.sqrt(jnp.sum(raw * raw, axis=1, keepdims=True) + EPSILON)
    inverse = 1.0 / length
    return raw * inverse, inverse


def project(direction, raw):
    unit, inverse = unit_of(raw)
    along = jnp.sum(unit * direction, axis=1, keepdims=True)
    return (direction - unit * along) * inverse


def kernel(
    groups,
    seq_hbm,
    st_hbm,
    lab_ref,
    scale_ref,
    bias_ref,
    loss_hbm,
    seq_out,
    st_out,
    stv,
    units,
    labs,
    columns,
    parts,
    backs,
    cross_back,
    acc,
    acc_in,
    losses,
    loss_backs,
    loss_cross,
    st_hi,
    st_lo,
    load_sem,
    acc_s,
    acc_r,
    cross_s,
    cross_r,
    ring_s,
    ring_r,
    lab_s,
    lab_r,
    back_s,
    back_r,
    xback_s,
    xback_r,
    loss_s,
    loss_r,
    loss_out,
    put_sem,
):
    half, features = seq_hbm.shape
    rows = half // CHUNKS
    piece = 2 * half // PIECES
    blk, rep = lax.axis_index("blk"), lax.axis_index("rep")
    core, x, group = blk % 2, (blk // 2) % RING, blk // (2 * RING)

    def at(g, column, replica):
        return ((lax.rem(g + groups, groups) * RING + lax.rem(column + RING, RING)) * 2 + core, replica)

    def ring(by):
        return at(group, x + by, rep)

    rep_up = lax.rem(rep + group + core, 2)
    rep_down = lax.rem(rep + group + 1 + core, 2)
    up = at(group + 1, x, rep_up)
    down = at(group - 1, x, rep_down)
    wraps = jnp.where(x == RING - 1, 1, 0)
    later = at(group + wraps, x + 1, jnp.where(x == RING - 1, rep_up, rep))
    wraps = jnp.where(x == 0, 1, 0)
    earlier = at(group - wraps, x - 1, jnp.where(x == 0, rep_down, rep))
    partner = (blk, 1 - rep)

    def send(src, dst, send_sem, recv_sem, device):
        return pltpu.make_async_remote_copy(
            src_ref=src, dst_ref=dst, send_sem=send_sem, recv_sem=recv_sem, device_id=device, device_id_type=MESH
        )

    def stays(h):
        return x < RING - h

    def leaves(h):
        return x >= RING - h

    def source(k):
        return seq_hbm.at[pl.ds(k * rows, rows)]

    fine = half // FINE

    def fresh(j):
        return seq_hbm.at[pl.ds(j * fine, fine)]

    def visitor(h, j):
        per = FINE // CHUNKS
        return units.at[j // per, h, pl.ds((j % per) * fine, fine)]

    def cross_copy(j):
        return send(fresh(j), visitor(HOPS, j), cross_s.at[j], cross_r.at[j], up)

    def ring_copy(h, j, crossed):
        src = visitor(HOPS, j) if crossed else fresh(j)
        return send(src, visitor(h, j), ring_s.at[h - 1, j], ring_r.at[h - 1, j], ring(h))

    def via(j):
        return 1 if j % 2 == 0 else 3

    def second_copy(j):
        device = later if via(j) == 1 else earlier
        return send(visitor(via(j), j), visitor(2, j), ring_s.at[1, j], ring_r.at[1, j], device)

    def label_copy(h, crossed):
        src = labs.at[HOPS if crossed else 0]
        return send(src, labs.at[h], lab_s.at[h - 1], lab_r.at[h - 1], up if h == HOPS else ring(h))

    def back_copy(h, k):
        return send(parts.at[k, h], backs.at[k, h - 1], back_s.at[h - 1, k], back_r.at[h - 1, k], ring(-h))

    def cross_back_copy(k):
        return send(parts.at[k, HOPS], cross_back.at[k], xback_s.at[k], xback_r.at[k], down)

    def loss_copy(h):
        dst = loss_cross if h == HOPS else loss_backs.at[h - 1]
        return send(losses.at[h], dst, loss_s.at[h - 1], loss_r.at[h - 1], down if h == HOPS else ring(-h))

    def acc_copy(p):
        here = pl.ds(p * piece, piece)
        return send(acc.at[here], acc_in.at[here], acc_s.at[p], acc_r.at[p], partner)

    load_st = pltpu.make_async_copy(st_hbm, stv, load_sem.at[0])
    load_seq = [pltpu.make_async_copy(source(k), units.at[k, 0], load_sem.at[1 + k]) for k in range(CHUNKS)]
    load_st.start()
    for copy in load_seq:
        copy.start()

    barrier = pltpu.get_barrier_semaphore()
    greeted = (ring(1), ring(2), ring(3), up, down, partner, later, earlier)
    for device in greeted:
        pl.semaphore_signal(barrier, 1, device_id=device, device_id_type=MESH)
    labs[0] = jnp.broadcast_to(lab_ref[pl.ds(rep, 1), :], (8, half))
    label_rows = [lab_ref[q : q + 1, :].astype(jnp.float32) for q in range(2)]
    pl.semaphore_wait(barrier, len(greeted))

    direct = (1, 3)

    def forward(k):
        for h in direct:

            @pl.when(stays(h))
            def _():
                ring_copy(h, k, False).start()

    def relay(k):
        cross_copy(k).wait_recv()
        for h in direct:

            @pl.when(leaves(h))
            def _():
                ring_copy(h, k, True).start()

    def second(k):
        ring_copy(via(k), k, False).wait_recv()
        second_copy(k).start()

    def arrived(k):
        for j in range(k * (FINE // CHUNKS), (k + 1) * (FINE // CHUNKS)):
            for h in TILES:
                if h != via(j):
                    ring_copy(h, j, False).wait_recv()

    def column(h):
        tall = jnp.broadcast_to(labs[h][0:1, :].astype(jnp.float32), (half, half)).T
        for k in range(CHUNKS):
            columns[k, h] = tall[k * rows : (k + 1) * rows]

    scale, bias = scale_ref[0], bias_ref[0]

    def back(k):
        for h in TILES:
            back_copy(h, k).start()

    def weigh(raw, label):
        seq = split(unit_of(raw)[0])
        st = (st_hi[...], st_lo[...])
        logit = scale * dot3(seq, st, ((1,), (1,))) + bias
        match = jnp.concatenate([label == label_rows[0], label == label_rows[1]], axis=1)
        margin = jnp.where(match, -logit, logit)
        small = jnp.exp(-jnp.abs(margin))
        loss = jnp.sum(jnp.maximum(margin, 0.0) + jnp.log1p(small), axis=1, keepdims=True)
        sigmoid = jnp.where(margin >= 0.0, 1.0, small) / (1.0 + small)
        weight = split(jnp.where(match, -sigmoid, sigmoid))
        return seq, weight, jnp.broadcast_to(loss, label.shape)

    def towards(weight, seq):
        return lax.dot_general(
            jnp.concatenate([weight[0], weight[1], weight[0]], axis=0),
            jnp.concatenate([seq[0], seq[0], seq[1]], axis=0),
            (((0,), (0,)), ((), ())),
            preferred_element_type=jnp.float32,
        )

    def away(weight):
        return dot3(weight, (st_hi[...], st_lo[...]), ((1,), (0,)))

    def whole(h):
        seq, weight, loss = weigh(
            jnp.concatenate([units[k, h] for k in range(CHUNKS)], axis=0),
            jnp.concatenate([columns[k, h] for k in range(CHUNKS)], axis=0),
        )
        result = away(weight)
        for k in range(CHUNKS):
            columns[k, h] = loss[k * rows : (k + 1) * rows]
            parts[k, h] = result[k * rows : (k + 1) * rows]
        if h == 0:
            acc[...] = towards(weight, seq)
        else:
            acc[...] += towards(weight, seq)

    visitors = pl.ds(1, RING - 1)

    def stage(k):
        arrived(k)
        seq, weight, loss = weigh(
            units[k, visitors].reshape((RING - 1) * rows, features), columns[k, visitors].reshape((RING - 1) * rows, half)
        )
        columns[k, visitors] = loss.reshape(RING - 1, rows, half)

        def send_back():
            parts[k, visitors] = away(weight).reshape(RING - 1, rows, features)
            back(k)

        if k < CHUNKS - 1:
            send_back()
        acc[...] += towards(weight, seq)
        if k == CHUNKS - 1:
            for p in range(PIECES):
                acc_copy(p).start()
            send_back()

    def collect(k):
        for h in TILES:

            @pl.when(leaves(h))
            def _():
                back_copy(h, k).wait_recv()
                parts[k, HOPS] += backs[k, h - 1]

        cross_back_copy(k).start()

    def finish(k):
        for h in TILES:

            @pl.when(stays(h))
            def _():
                back_copy(h, k).wait_recv()
                parts[k, 0] += backs[k, h - 1]

        cross_back_copy(k).wait_recv()
        parts[k, 0] = project(scale * (parts[k, 0] + cross_back[k]), units[k, 0])
        put_seq(k).start()

    put_loss = pltpu.make_async_copy(loss_out, loss_hbm, put_sem.at[0])

    def put_seq(k):
        return pltpu.make_async_copy(parts.at[k, 0], seq_out.at[pl.ds(k * rows, rows)], put_sem.at[1 + k])

    def put_st(p):
        here = pl.ds(p * piece, piece)
        return pltpu.make_async_copy(acc_in.at[here], st_out.at[here], put_sem.at[1 + CHUNKS + p])

    def settle(p):
        here = pl.ds(p * piece, piece)
        acc_copy(p).wait_recv()
        acc_in[here] = project(scale * (acc[here] + acc_in[here]), stv[here])
        put_st(p).start()

    label_copy(HOPS, False).start()
    for h in TILES:

        @pl.when(stays(h))
        def _():
            label_copy(h, False).start()

    for k in range(FINE):
        cross_copy(k).start()
    for k in range(FINE):
        forward(k)

    column(0)
    load_st.wait()
    unit, _ = unit_of(stv[...])
    st_hi[...], st_lo[...] = split(unit)
    for copy in load_seq:
        copy.wait()
    whole(0)
    label_copy(HOPS, False).wait_recv()
    for h in TILES:

        @pl.when(leaves(h))
        def _():
            label_copy(h, True).start()

    column(HOPS)
    for k in range(FINE):
        relay(k)
        if k >= 4:
            second(k - 4)
    for h in TILES:
        label_copy(h, False).wait_recv()
        column(h)
    for k in range(4, FINE):
        if k == FOURTH + 2:
            whole(HOPS)
        second(k)
    for k in range(CHUNKS):
        stage(k)

    for k in range(CHUNKS):
        collect(k)
        if k == 0:
            for h in range(HOPS + 1):
                tall = jnp.concatenate([columns[k, h] for k in range(CHUNKS)], axis=0)
                losses[h] = tall.T[0:8, :]
            for h in TILES:
                loss_copy(h).start()
        if k == 2:
            for h in TILES:
                loss_copy(h).wait_recv()
            gone = losses[HOPS]
            kept = losses[0]
            for h in TILES:
                gone += jnp.where(leaves(h), loss_backs[h - 1], 0.0)
                kept += jnp.where(stays(h), loss_backs[h - 1], 0.0)
            losses[HOPS] = gone
            loss_copy(HOPS).start()
    for p in range(PIECES):
        settle(p)
    for k in range(CHUNKS):
        finish(k)
    loss_copy(HOPS).wait_recv()
    loss_out[...] = (kept[0:1, :] + loss_cross[0:1, :]) / ((HOPS + 1) * 2.0 * half)
    put_loss.start()

    for j in range(FINE):
        cross_copy(j).wait_send()
        for h in TILES:
            ring_copy(h, j, False).wait_send()
    for k in range(CHUNKS):
        cross_back_copy(k).wait_send()
        for h in TILES:
            back_copy(h, k).wait_send()
    for h in TILES + (HOPS,):
        label_copy(h, False).wait_send()
        loss_copy(h).wait_send()
    for p in range(PIECES):
        acc_copy(p).wait_send()
        put_st(p).wait()
    for k in range(CHUNKS):
        put_seq(k).wait()
    put_loss.wait()


def hand_over(a, b, c, p, q, r, sa, sb, sc, sem):
    moves = [(a, sa, p, slice(None)), (b, sb, q, slice(None))]
    half = b.shape[0]
    moves += [(c, sc, r, pl.ds(i * half, half)) for i in range(2)]
    ins = [pltpu.make_async_copy(s.at[w], v.at[w], sem.at[0, i]) for i, (s, v, _, w) in enumerate(moves)]
    outs = [pltpu.make_async_copy(v.at[w], d.at[w], sem.at[1, i]) for i, (_, v, d, w) in enumerate(moves)]
    for copy in ins:
        copy.start()
    for into, out in zip(ins, outs):
        into.wait()
        out.start()
    for copy in outs:
        copy.wait()


def body(seq, st, label, scale, bias):
    half, features = seq.shape
    rows = half // CHUNKS
    f32, bf16 = jnp.float32, jnp.bfloat16
    vmem, dma = pltpu.VMEM, pltpu.SemaphoreType.DMA
    groups = lax.axis_size("blk") // (2 * RING)
    loss, seq_grad, st_grad = pl.pallas_call(
        functools.partial(kernel, groups),
        out_shape=(
            jax.ShapeDtypeStruct((1, half), f32),
            jax.ShapeDtypeStruct(seq.shape, f32),
            jax.ShapeDtypeStruct(st.shape, f32),
        ),
        in_specs=[
            pl.BlockSpec(memory_space=pl.ANY),
            pl.BlockSpec(memory_space=pl.ANY),
            pl.BlockSpec(memory_space=vmem),
            pl.BlockSpec(memory_space=pltpu.SMEM),
            pl.BlockSpec(memory_space=pltpu.SMEM),
        ],
        out_specs=(pl.BlockSpec(memory_space=pl.ANY),) * 3,
        scratch_shapes=[
            vmem((2 * half, features), f32),
            vmem((CHUNKS, HOPS + 1, rows, features), f32),
            vmem((HOPS + 1, 8, half), jnp.int32),
            vmem((CHUNKS, HOPS + 1, rows, half), f32),
            vmem((CHUNKS, HOPS + 1, rows, features), f32),
            vmem((CHUNKS, RING - 1, rows, features), f32),
            vmem((CHUNKS, rows, features), f32),
            vmem((2 * half, features), f32),
            vmem((2 * half, features), f32),
            vmem((HOPS + 1, 8, half), f32),
            vmem((RING - 1, 8, half), f32),
            vmem((8, half), f32),
            vmem((2 * half, features), bf16),
            vmem((2 * half, features), bf16),
            dma((1 + CHUNKS,)),
            dma((PIECES,)),
            dma((PIECES,)),
            dma((FINE,)),
            dma((FINE,)),
            dma((RING - 1, FINE)),
            dma((RING - 1, FINE)),
            dma((HOPS,)),
            dma((HOPS,)),
            dma((RING - 1, CHUNKS)),
            dma((RING - 1, CHUNKS)),
            dma((CHUNKS,)),
            dma((CHUNKS,)),
            dma((HOPS,)),
            dma((HOPS,)),
            vmem((1, half), f32),
            dma((1 + CHUNKS + PIECES,)),
        ],
        compiler_params=pltpu.CompilerParams(
            collective_id=1, has_side_effects=True, vmem_limit_bytes=56 * 2**20
        ),
    )(seq, st, label.reshape(2, half), scale, bias)
    loss, seq_grad, st_grad = pl.pallas_call(
        hand_over,
        out_shape=(
            jax.ShapeDtypeStruct((1, half), f32),
            jax.ShapeDtypeStruct(seq.shape, f32),
            jax.ShapeDtypeStruct(st.shape, f32),
        ),
        in_specs=[pl.BlockSpec(memory_space=pl.ANY)] * 3,
        out_specs=(pl.BlockSpec(memory_space=pl.ANY),) * 3,
        scratch_shapes=[vmem((1, half), f32), vmem(seq.shape, f32), vmem(st.shape, f32), dma((2, 4))],
        name="hand_over",
    )(loss, seq_grad, st_grad)
    return loss.reshape(half), seq_grad, st_grad


def solution(mesh):
    placed = (P(("blk", "rep"), None), P("blk", None), P("blk"), P(), P())
    return jax.shard_map(
        body,
        mesh=mesh,
        in_specs=placed,
        out_specs=(P(("blk", "rep")), P(("blk", "rep"), None), P("blk", None)),
        check_vma=False,
    )
```

```python
import functools

import jax
import jax.numpy as jnp
from jax import lax
from jax.experimental import pallas as pl
from jax.experimental.pallas import tpu as pltpu
from jax.sharding import PartitionSpec as P

MESH = pl.DeviceIdType.MESH
HOPS = 4
EPSILON = 1e-06
CHUNKS = 4
RING = 4
TILES = (3, 2, 1)
PIECES = 4
FINE = 8
FOURTH = 4


def split(value):
    high = value.astype(jnp.bfloat16)
    return high, (value - high.astype(jnp.float32)).astype(jnp.bfloat16)


def dot3(a, b, dims):
    def one(p, q):
        return lax.dot_general(p, q, (dims, ((), ())), preferred_element_type=jnp.float32)

    return one(a[0], b[0]) + one(a[0], b[1]) + one(a[1], b[0])


def unit_of(raw):
    length = jnp.sqrt(jnp.sum(raw * raw, axis=1, keepdims=True) + EPSILON)
    inverse = 1.0 / length
    return raw * inverse, inverse


def project(direction, raw):
    unit, inverse = unit_of(raw)
    along = jnp.sum(unit * direction, axis=1, keepdims=True)
    return (direction - unit * along) * inverse


def kernel(
    groups,
    seq_hbm,
    st_hbm,
    lab_ref,
    scale_ref,
    bias_ref,
    loss_hbm,
    seq_out,
    st_out,
    stv,
    units,
    labs,
    columns,
    parts,
    backs,
    cross_back,
    acc,
    acc_in,
    losses,
    loss_backs,
    loss_cross,
    st_hi,
    st_lo,
    load_sem,
    acc_s,
    acc_r,
    cross_s,
    cross_r,
    ring_s,
    ring_r,
    lab_s,
    lab_r,
    back_s,
    back_r,
    xback_s,
    xback_r,
    loss_s,
    loss_r,
    loss_out,
    put_sem,
):
    half, features = seq_hbm.shape
    rows = half // CHUNKS
    piece = 2 * half // PIECES
    blk, rep = lax.axis_index("blk"), lax.axis_index("rep")
    core, x, group = blk % 2, (blk // 2) % RING, blk // (2 * RING)

    def at(g, column, replica):
        return ((lax.rem(g + groups, groups) * RING + lax.rem(column + RING, RING)) * 2 + core, replica)

    def ring(by):
        return at(group, x + by, rep)

    rep_up = lax.rem(rep + group + core, 2)
    rep_down = lax.rem(rep + group + 1 + core, 2)
    up = at(group + 1, x, rep_up)
    down = at(group - 1, x, rep_down)
    wraps = jnp.where(x == RING - 1, 1, 0)
    later = at(group + wraps, x + 1, jnp.where(x == RING - 1, rep_up, rep))
    wraps = jnp.where(x == 0, 1, 0)
    earlier = at(group - wraps, x - 1, jnp.where(x == 0, rep_down, rep))
    partner = (blk, 1 - rep)

    def send(src, dst, send_sem, recv_sem, device):
        return pltpu.make_async_remote_copy(
            src_ref=src, dst_ref=dst, send_sem=send_sem, recv_sem=recv_sem, device_id=device, device_id_type=MESH
        )

    def stays(h):
        return x < RING - h

    def leaves(h):
        return x >= RING - h

    def source(k):
        return seq_hbm.at[pl.ds(k * rows, rows)]

    fine = half // FINE

    def fresh(j):
        return seq_hbm.at[pl.ds(j * fine, fine)]

    def visitor(h, j):
        per = FINE // CHUNKS
        return units.at[j // per, h, pl.ds((j % per) * fine, fine)]

    def cross_copy(j):
        return send(fresh(j), visitor(HOPS, j), cross_s.at[j], cross_r.at[j], up)

    def ring_copy(h, j, crossed):
        src = visitor(HOPS, j) if crossed else fresh(j)
        return send(src, visitor(h, j), ring_s.at[h - 1, j], ring_r.at[h - 1, j], ring(h))

    def via(j):
        return 1 if j % 2 == 0 else 3

    def second_copy(j):
        device = later if via(j) == 1 else earlier
        return send(visitor(via(j), j), visitor(2, j), ring_s.at[1, j], ring_r.at[1, j], device)

    def label_copy(h, crossed):
        src = labs.at[HOPS if crossed else 0]
        return send(src, labs.at[h], lab_s.at[h - 1], lab_r.at[h - 1], up if h == HOPS else ring(h))

    def back_copy(h, k):
        return send(parts.at[k, h], backs.at[k, h - 1], back_s.at[h - 1, k], back_r.at[h - 1, k], ring(-h))

    def cross_back_copy(k):
        return send(parts.at[k, HOPS], cross_back.at[k], xback_s.at[k], xback_r.at[k], down)

    def loss_copy(h):
        dst = loss_cross if h == HOPS else loss_backs.at[h - 1]
        return send(losses.at[h], dst, loss_s.at[h - 1], loss_r.at[h - 1], down if h == HOPS else ring(-h))

    def acc_copy(p):
        here = pl.ds(p * piece, piece)
        return send(acc.at[here], acc_in.at[here], acc_s.at[p], acc_r.at[p], partner)

    load_st = pltpu.make_async_copy(st_hbm, stv, load_sem.at[0])
    load_seq = [pltpu.make_async_copy(source(k), units.at[k, 0], load_sem.at[1 + k]) for k in range(CHUNKS)]
    load_st.start()
    for copy in load_seq:
        copy.start()

    barrier = pltpu.get_barrier_semaphore()
    greeted = (ring(1), ring(2), ring(3), up, down, partner, later, earlier)
    for device in greeted:
        pl.semaphore_signal(barrier, 1, device_id=device, device_id_type=MESH)
    labs[0] = jnp.broadcast_to(lab_ref[pl.ds(rep, 1), :], (8, half))
    label_rows = [lab_ref[q : q + 1, :].astype(jnp.float32) for q in range(2)]
    pl.semaphore_wait(barrier, len(greeted))

    direct = (1, 3)

    def forward(k):
        for h in direct:

            @pl.when(stays(h))
            def _():
                ring_copy(h, k, False).start()

    def relay(k):
        cross_copy(k).wait_recv()
        for h in direct:

            @pl.when(leaves(h))
            def _():
                ring_copy(h, k, True).start()

    def second(k):
        ring_copy(via(k), k, False).wait_recv()
        second_copy(k).start()

    def arrived(k):
        for j in range(k * (FINE // CHUNKS), (k + 1) * (FINE // CHUNKS)):
            for h in TILES:
                if h != via(j):
                    ring_copy(h, j, False).wait_recv()

    def column(h):
        tall = jnp.broadcast_to(labs[h][0:1, :].astype(jnp.float32), (half, half)).T
        for k in range(CHUNKS):
            columns[k, h] = tall[k * rows : (k + 1) * rows]

    scale, bias = scale_ref[0], bias_ref[0]

    def back(k):
        for h in TILES:
            back_copy(h, k).start()

    def weigh(raw, label):
        seq = split(unit_of(raw)[0])
        st = (st_hi[...], st_lo[...])
        logit = scale * dot3(seq, st, ((1,), (1,))) + bias
        match = jnp.concatenate([label == label_rows[0], label == label_rows[1]], axis=1)
        margin = jnp.where(match, -logit, logit)
        small = jnp.exp(-jnp.abs(margin))
        loss = jnp.sum(jnp.maximum(margin, 0.0) + jnp.log1p(small), axis=1, keepdims=True)
        sigmoid = jnp.where(margin >= 0.0, 1.0, small) / (1.0 + small)
        weight = split(jnp.where(match, -sigmoid, sigmoid))
        return seq, weight, jnp.broadcast_to(loss, label.shape)

    def towards(weight, seq):
        return lax.dot_general(
            jnp.concatenate([weight[0], weight[1], weight[0]], axis=0),
            jnp.concatenate([seq[0], seq[0], seq[1]], axis=0),
            (((0,), (0,)), ((), ())),
            preferred_element_type=jnp.float32,
        )

    def away(weight):
        return dot3(weight, (st_hi[...], st_lo[...]), ((1,), (0,)))

    def whole(h):
        seq, weight, loss = weigh(
            jnp.concatenate([units[k, h] for k in range(CHUNKS)], axis=0),
            jnp.concatenate([columns[k, h] for k in range(CHUNKS)], axis=0),
        )
        result = away(weight)
        for k in range(CHUNKS):
            columns[k, h] = loss[k * rows : (k + 1) * rows]
            parts[k, h] = result[k * rows : (k + 1) * rows]
        if h == 0:
            acc[...] = towards(weight, seq)
        else:
            acc[...] += towards(weight, seq)

    visitors = pl.ds(1, RING - 1)

    def stage(k):
        arrived(k)
        seq, weight, loss = weigh(
            units[k, visitors].reshape((RING - 1) * rows, features), columns[k, visitors].reshape((RING - 1) * rows, half)
        )
        columns[k, visitors] = loss.reshape(RING - 1, rows, half)

        def send_back():
            parts[k, visitors] = away(weight).reshape(RING - 1, rows, features)
            back(k)

        send_back()
        acc[...] += towards(weight, seq)
        if k == CHUNKS - 1:
            for p in range(PIECES):
                acc_copy(p).start()

    def collect(k):
        for h in TILES:

            @pl.when(leaves(h))
            def _():
                back_copy(h, k).wait_recv()
                parts[k, HOPS] += backs[k, h - 1]

        cross_back_copy(k).start()

    def finish(k):
        for h in TILES:

            @pl.when(stays(h))
            def _():
                back_copy(h, k).wait_recv()
                parts[k, 0] += backs[k, h - 1]

        cross_back_copy(k).wait_recv()
        parts[k, 0] = project(scale * (parts[k, 0] + cross_back[k]), units[k, 0])
        put_seq(k).start()

    put_loss = pltpu.make_async_copy(loss_out, loss_hbm, put_sem.at[0])

    def put_seq(k):
        return pltpu.make_async_copy(parts.at[k, 0], seq_out.at[pl.ds(k * rows, rows)], put_sem.at[1 + k])

    def put_st(p):
        here = pl.ds(p * piece, piece)
        return pltpu.make_async_copy(acc_in.at[here], st_out.at[here], put_sem.at[1 + CHUNKS + p])

    def settle(p):
        here = pl.ds(p * piece, piece)
        acc_copy(p).wait_recv()
        acc_in[here] = project(scale * (acc[here] + acc_in[here]), stv[here])
        put_st(p).start()

    label_copy(HOPS, False).start()
    for h in TILES:

        @pl.when(stays(h))
        def _():
            label_copy(h, False).start()

    for k in range(FINE):
        cross_copy(k).start()
    for k in range(FINE):
        forward(k)

    column(0)
    load_st.wait()
    unit, _ = unit_of(stv[...])
    st_hi[...], st_lo[...] = split(unit)
    for copy in load_seq:
        copy.wait()
    label_copy(HOPS, False).wait_recv()
    for h in TILES:

        @pl.when(leaves(h))
        def _():
            label_copy(h, True).start()

    column(HOPS)
    for k in range(FINE):
        relay(k)
        if k == 1:
            whole(0)
        if k >= 4:
            second(k - 4)
    for h in TILES:
        label_copy(h, False).wait_recv()
        column(h)
    for k in range(4, FINE):
        if k == FOURTH + 2:
            whole(HOPS)
        second(k)
    for k in range(CHUNKS):
        stage(k)

    for k in range(CHUNKS):
        collect(k)
        if k == 0:
            for h in range(HOPS + 1):
                tall = jnp.concatenate([columns[k, h] for k in range(CHUNKS)], axis=0)
                losses[h] = tall.T[0:8, :]
            for h in TILES:
                loss_copy(h).start()
        if k == 2:
            for h in TILES:
                loss_copy(h).wait_recv()
            gone = losses[HOPS]
            kept = losses[0]
            for h in TILES:
                gone += jnp.where(leaves(h), loss_backs[h - 1], 0.0)
                kept += jnp.where(stays(h), loss_backs[h - 1], 0.0)
            losses[HOPS] = gone
            loss_copy(HOPS).start()
    for p in range(PIECES):
        settle(p)
    for k in range(CHUNKS):
        finish(k)
    loss_copy(HOPS).wait_recv()
    loss_out[...] = (kept[0:1, :] + loss_cross[0:1, :]) / ((HOPS + 1) * 2.0 * half)
    put_loss.start()

    for j in range(FINE):
        cross_copy(j).wait_send()
        for h in TILES:
            ring_copy(h, j, False).wait_send()
    for k in range(CHUNKS):
        cross_back_copy(k).wait_send()
        for h in TILES:
            back_copy(h, k).wait_send()
    for h in TILES + (HOPS,):
        label_copy(h, False).wait_send()
        loss_copy(h).wait_send()
    for p in range(PIECES):
        acc_copy(p).wait_send()
        put_st(p).wait()
    for k in range(CHUNKS):
        put_seq(k).wait()
    put_loss.wait()


def hand_over(a, b, c, p, q, r, sa, sb, sc, sem):
    moves = [(a, sa, p, slice(None)), (b, sb, q, slice(None))]
    half = b.shape[0]
    moves += [(c, sc, r, pl.ds(i * half, half)) for i in range(2)]
    ins = [pltpu.make_async_copy(s.at[w], v.at[w], sem.at[0, i]) for i, (s, v, _, w) in enumerate(moves)]
    outs = [pltpu.make_async_copy(v.at[w], d.at[w], sem.at[1, i]) for i, (_, v, d, w) in enumerate(moves)]
    for copy in ins:
        copy.start()
    for into, out in zip(ins, outs):
        into.wait()
        out.start()
    for copy in outs:
        copy.wait()


def body(seq, st, label, scale, bias):
    half, features = seq.shape
    rows = half // CHUNKS
    f32, bf16 = jnp.float32, jnp.bfloat16
    vmem, dma = pltpu.VMEM, pltpu.SemaphoreType.DMA
    groups = lax.axis_size("blk") // (2 * RING)
    loss, seq_grad, st_grad = pl.pallas_call(
        functools.partial(kernel, groups),
        out_shape=(
            jax.ShapeDtypeStruct((1, half), f32),
            jax.ShapeDtypeStruct(seq.shape, f32),
            jax.ShapeDtypeStruct(st.shape, f32),
        ),
        in_specs=[
            pl.BlockSpec(memory_space=pl.ANY),
            pl.BlockSpec(memory_space=pl.ANY),
            pl.BlockSpec(memory_space=vmem),
            pl.BlockSpec(memory_space=pltpu.SMEM),
            pl.BlockSpec(memory_space=pltpu.SMEM),
        ],
        out_specs=(pl.BlockSpec(memory_space=pl.ANY),) * 3,
        scratch_shapes=[
            vmem((2 * half, features), f32),
            vmem((CHUNKS, HOPS + 1, rows, features), f32),
            vmem((HOPS + 1, 8, half), jnp.int32),
            vmem((CHUNKS, HOPS + 1, rows, half), f32),
            vmem((CHUNKS, HOPS + 1, rows, features), f32),
            vmem((CHUNKS, RING - 1, rows, features), f32),
            vmem((CHUNKS, rows, features), f32),
            vmem((2 * half, features), f32),
            vmem((2 * half, features), f32),
            vmem((HOPS + 1, 8, half), f32),
            vmem((RING - 1, 8, half), f32),
            vmem((8, half), f32),
            vmem((2 * half, features), bf16),
            vmem((2 * half, features), bf16),
            dma((1 + CHUNKS,)),
            dma((PIECES,)),
            dma((PIECES,)),
            dma((FINE,)),
            dma((FINE,)),
            dma((RING - 1, FINE)),
            dma((RING - 1, FINE)),
            dma((HOPS,)),
            dma((HOPS,)),
            dma((RING - 1, CHUNKS)),
            dma((RING - 1, CHUNKS)),
            dma((CHUNKS,)),
            dma((CHUNKS,)),
            dma((HOPS,)),
            dma((HOPS,)),
            vmem((1, half), f32),
            dma((1 + CHUNKS + PIECES,)),
        ],
        compiler_params=pltpu.CompilerParams(
            collective_id=1, has_side_effects=True, vmem_limit_bytes=56 * 2**20
        ),
    )(seq, st, label.reshape(2, half), scale, bias)
    loss, seq_grad, st_grad = pl.pallas_call(
        hand_over,
        out_shape=(
            jax.ShapeDtypeStruct((1, half), f32),
            jax.ShapeDtypeStruct(seq.shape, f32),
            jax.ShapeDtypeStruct(st.shape, f32),
        ),
        in_specs=[pl.BlockSpec(memory_space=pl.ANY)] * 3,
        out_specs=(pl.BlockSpec(memory_space=pl.ANY),) * 3,
        scratch_shapes=[vmem((1, half), f32), vmem(seq.shape, f32), vmem(st.shape, f32), dma((2, 4))],
        name="hand_over",
    )(loss, seq_grad, st_grad)
    return loss.reshape(half), seq_grad, st_grad


def solution(mesh):
    placed = (P(("blk", "rep"), None), P("blk", None), P("blk"), P(), P())
    return jax.shard_map(
        body,
        mesh=mesh,
        in_specs=placed,
        out_specs=(P(("blk", "rep")), P(("blk", "rep"), None), P("blk", None)),
        check_vma=False,
    )
```
